32 devices in a mesh: groups: 2 (over x), ctx: 16 (over z, y, core).
Axes of the slice: x: 2, y: 2, z: 4, core: 2. Of those that a mesh axis runs over, the one named last changes fastest.
Arguments:
- mr_qkv: bfloat16 [16384, 12288], P(('groups', 'ctx')), parts along dimension 0, may hold values from -6 to 6
- mr_filter: bfloat16 [256, 128], replicated, may hold values from -0.5 to 0.5
- li_gates: bfloat16 [16384, 8192], P(('groups', 'ctx')), parts along dimension 0, may hold values from -6 to 6
- decay: float32 [4096, 16], replicated, may hold values from 2.4414063e-05 to 0.0333333333
- residue: float32 [4096, 16], replicated, may hold values from -1.8144368 to 1.8144368
Outputs:
- mixer_out: bfloat16 [16384, 4096], P(('groups', 'ctx')), parts along dimension 0
The draws below stay inside these ranges and needn't reach their ends.
There are 2 independent parts, one for each index of `groups`. The reference program is written for one: setup_inputs(seed, part) draws one part's arguments, and reference() takes and returns one part's arrays. A program takes and returns all parts, laid end to end along the dimension named above; an argument that names none is the same for every part. Nothing has to cross between parts.
All inputs are finite; a program needn't handle non-finite values.
Results may differ from the reference program's by a relative error of at most 0.005.
Values may be sent and summed in bfloat16 or wider, within the bound.
A program may use at most 384 MiB of HBM per device.

```python
import jax
import jax.numpy as jnp
from jax import lax

D = 4096
FLEN = 128
NMODE = 16
GROUP = 16
G = 256
SEQ = 8192


def draw_modes(key):
    base_key = jax.random.fold_in(key, 7)
    pick_key, slow_key, fast_key, gap_key = jax.random.split(base_key, 4)
    pair_shape = (D, NMODE // 2)
    slow_share = 0.5
    choose = jax.random.uniform(pick_key, pair_shape, jnp.float32) < slow_share
    slow_rates = jnp.exp(jax.random.uniform(slow_key, pair_shape, jnp.float32, jnp.log(0.2 / SEQ), jnp.log(1.2 / SEQ)))
    fast_rates = jnp.exp(jax.random.uniform(fast_key, pair_shape, jnp.float32, jnp.log(2.0 / SEQ), jnp.log(1.0 / 54)))
    base_rates = jnp.where(choose, slow_rates, fast_rates)
    gaps = jax.random.uniform(gap_key, pair_shape, jnp.float32, 0.3, 0.8)
    return (base_rates, gaps)


def draw_decay(key, part):
    base_rates, gaps = draw_modes(key)
    paired = jnp.stack([base_rates, base_rates * (1.0 + gaps)], axis=2)
    return paired.reshape(D, NMODE)


def draw_residue(key, part):
    base_rates, gaps = draw_modes(key)
    pair_shape = (D, NMODE // 2)
    noise = jnp.clip(jax.random.normal(jax.random.fold_in(key, 11), pair_shape, jnp.float32), -4.0, 4.0)
    ratio = jax.random.uniform(jax.random.fold_in(key, 13), pair_shape, jnp.float32, 0.95, 1.0)
    leading = noise * 4.0 * jnp.sqrt(base_rates / NMODE) / gaps
    paired = jnp.stack([leading, -ratio * leading], axis=2)
    return paired.reshape(D, NMODE)


def steps_of(key, shape, cuts, low, largest):
    def one(position, blocks):
        draws = jax.random.uniform(jax.random.fold_in(jax.random.fold_in(key, 6), position), (blocks,), jnp.float32, low / len(cuts), largest / len(cuts))
        return jnp.repeat(jnp.exp(draws), shape[position] // blocks).reshape((-1,) + (1,) * (len(shape) - position - 1))

    level = one(*cuts[0])
    for cut in cuts[1:]:
        level = level * one(*cut)
    return level


def centred(own_key, dims, width, reach, cuts=(), kind=jnp.bfloat16):
    factor_of = steps_of(own_key, dims, cuts, -0.22, 0.18) if cuts else 1.0
    values = jax.random.normal(own_key, dims, jnp.float32) * width * factor_of
    return jnp.minimum(jnp.maximum(values, -reach), reach).astype(kind)


def setup_inputs(seed: int = 0, part: int = 0) -> dict:
    splits = jax.random.split(jax.random.key(seed), 6)
    part_keys = jax.random.split(jax.random.fold_in(splits[5], part), 6)
    return {
        "mr_qkv": centred(part_keys[0], (SEQ, 3 * D), 1.0, 6.0, ((0, 16),)),
        "mr_filter": centred(splits[1], (G, FLEN), FLEN ** -0.5, 0.5),
        "li_gates": centred(part_keys[2], (SEQ, 2 * D), 1.0, 6.0, ((0, 16),)),
        "decay": draw_decay(jax.random.fold_in(splits[5], 71), part),
        "residue": draw_residue(jax.random.fold_in(splits[5], 71), part),
    }


def causal_product(signal, kernel):
    length = signal.shape[0]
    spectrum = jnp.fft.rfft(signal, n=2 * length, axis=0) * jnp.fft.rfft(kernel, n=2 * length, axis=0)
    return jnp.fft.irfft(spectrum, n=2 * length, axis=0)[:length]


def reference(mr_qkv, mr_filter, li_gates, decay, residue):
    query_mr = mr_qkv[:, :D].astype(jnp.float32)
    key_mr = mr_qkv[:, D:2 * D].astype(jnp.float32)
    value_mr = mr_qkv[:, 2 * D:].astype(jnp.float32)
    query_li = li_gates[:, :D].astype(jnp.float32)
    key_li = li_gates[:, D:].astype(jnp.float32)
    product_mr = (key_mr * value_mr).astype(jnp.bfloat16)
    product_mr = lax.optimization_barrier(product_mr).astype(jnp.float32)
    filter_taps = jnp.repeat(mr_filter.astype(jnp.float32), GROUP, axis=0)
    short_kernel = jnp.pad(filter_taps.T, ((0, SEQ - FLEN), (0, 0)))
    block_width = min(D, 128)
    block_total = D // block_width

    def split_cols(array):
        return array.reshape(SEQ, block_total, block_width).transpose(1, 0, 2)

    offsets = jnp.arange(SEQ, dtype=jnp.float32)

    def channel_block(inputs):
        query_one, product_one, kernel_one, key_two, query_two, decay_one, residue_one = inputs
        convolved = causal_product(product_one, kernel_one)
        li_input = key_two * (query_one * convolved)
        li_filter = jnp.sum(residue_one[None] * jnp.exp(-decay_one[None] * offsets[:, None, None]), axis=2)
        long_conv = causal_product(li_input, li_filter)
        return query_two * long_conv

    results = lax.map(channel_block, (split_cols(query_mr), split_cols(product_mr), split_cols(short_kernel), split_cols(key_li), split_cols(query_li), decay.reshape(block_total, block_width, NMODE), residue.reshape(block_total, block_width, NMODE)))
    return results.transpose(1, 0, 2).reshape(SEQ, D).astype(jnp.bfloat16)
```

```python
import functools

import jax
import jax.numpy as jnp
import numpy as np
from jax import lax
from jax.experimental import pallas as pl
from jax.experimental.pallas import tpu as pltpu
from jax.sharding import PartitionSpec as P

F32 = jnp.float32
BF16 = jnp.bfloat16
LEN = 128
NODES = 16
FAR_NODES = 32


def halves(table):
    high = table.astype(BF16)
    low = (table - high.astype(np.float64)).astype(BF16)
    return high, low


def lagrange(length, count):
    angle = (2 * np.arange(count) + 1) * np.pi / (2 * count)
    unit = np.cos(angle)
    weight = (-1.0) ** np.arange(count) * np.sin(angle)
    middle = (length - 1) / 2
    points = (np.arange(length) - middle) / middle
    gap = points[:, None] - unit[None, :]
    hit = np.abs(gap) < 1e-14
    ratio = weight[None, :] / np.where(hit, 1.0, gap)
    basis = ratio / ratio.sum(axis=1, keepdims=True)
    rows = hit.any(axis=1)
    basis[rows] = hit[rows]
    return middle + middle * unit, basis


def tables(width):
    freq = np.concatenate([np.arange(0, LEN, 2), np.arange(1, LEN, 2)])
    theta = np.pi * (freq[:, None] + 0.5) * np.arange(LEN)[None, :] / LEN
    forward = np.concatenate([np.cos(theta), -np.sin(theta)], axis=0)
    inverse = (forward.T / LEN).astype(BF16)
    nodes, basis = lagrange(LEN, NODES)
    fwd = np.concatenate([forward, basis[::-1].T], axis=0)
    fwd = np.concatenate(halves(fwd), axis=1)
    tap_high, tap_low = halves(forward @ basis)
    taps = np.concatenate([tap_high, tap_low, tap_high], axis=1)
    near_high, near_low = halves(basis)
    near = np.concatenate([near_high, near_low, near_high], axis=1)
    group = np.arange(width)[None, :] // 16 == np.arange(width // 16)[:, None]
    return nodes, fwd, inverse, taps, near, group


def dot(a, b):
    return lax.dot_general(a, b, (((1,), (0,)), ((), ())), preferred_element_type=F32)


def tripled(values):
    high = values.astype(BF16)
    low = (values - high.astype(F32)).astype(BF16)
    return jnp.concatenate([high, high, low], axis=0)


def twice(values):
    return jnp.concatenate([values, values], axis=0)


def times(re, im, filter_re, filter_im):
    return jnp.concatenate(
        [
            (re * filter_re - im * filter_im).astype(BF16),
            (re * filter_im + im * filter_re).astype(BF16),
        ],
        axis=0,
    )


def column(values):
    rows = lax.broadcasted_iota(jnp.int32, (len(values), 1), 0)
    total = jnp.zeros((len(values), 1), F32)
    for k, value in enumerate(values):
        total = jnp.where(rows == k, np.float32(value), total)
    return total


def near_kernel(
    nodes, q_ref, k_ref, v_ref, halo_ref, key_ref, filt_ref, decay_ref, residue_ref,
    fwd_ref, inv_ref, taps_ref, near_ref, group_ref, out_ref, sum_ref,
):
    blocks = q_ref.shape[0] // LEN
    half = LEN // 2
    modes = decay_ref.shape[0]
    fwd_all = fwd_ref[...]
    fwd = fwd_all[: 2 * LEN]
    inv = inv_ref[...]
    decay = decay_ref[...]
    residue = residue_ref[...]
    width = decay.shape[1]
    node_col = column(nodes)

    def at_nodes(weights):
        total = None
        for m in range(modes):
            part = node_rows[m] * weights[m : m + 1]
            total = part if total is None else total + part
        return total

    node_rows = [jnp.exp(-node_col * decay[m : m + 1]) for m in range(modes)]
    mode_rows = [jnp.exp(-np.float32(node) * decay) for node in nodes]
    weight = residue * jnp.exp(-decay)
    step = jnp.exp(-np.float32(LEN) * decay)

    expanded = lax.dot_general(
        filt_ref[...], group_ref[...], (((0,), (0,)), ((), ())), preferred_element_type=F32
    ).astype(BF16)
    short = dot(fwd, twice(expanded))
    short_re, short_im = short[:LEN], short[LEN:]
    long = dot(taps_ref[...], tripled(at_nodes(residue)))
    long_re, long_im = long[:LEN], long[LEN:]

    before = dot(fwd, twice(halo_ref[...]))
    state = None
    for i in range(blocks):
        rows = pl.ds(i * LEN, LEN)
        product = (k_ref[rows, :].astype(F32) * v_ref[rows, :].astype(F32)).astype(BF16)
        now = dot(fwd, twice(product))
        turned_re = jnp.concatenate(
            [
                now[:half] - before[LEN : LEN + half],
                now[half:LEN] + before[LEN + half :],
            ],
            axis=0,
        )
        turned_im = jnp.concatenate(
            [
                now[LEN : LEN + half] + before[:half],
                now[LEN + half :] - before[half:LEN],
            ],
            axis=0,
        )
        convolved = dot(inv, times(turned_re, turned_im, short_re, short_im))
        before = now
        li_input = key_ref[rows, :].astype(F32) * (q_ref[rows, :].astype(F32) * convolved)
        seen = dot(fwd_all, twice(li_input.astype(BF16)))
        value = dot(inv, times(seen[:LEN], seen[LEN : 2 * LEN], long_re, long_im))
        if state is not None:
            value = value + dot(near_ref[...], tripled(at_nodes(weight * state)))
        out_ref[rows, :] = value
        ended = None
        for k in range(len(nodes)):
            part = mode_rows[k] * seen[2 * LEN + k : 2 * LEN + k + 1]
            ended = part if ended is None else ended + part
        state = ended if state is None else step * state + ended
    sum_ref[...] = state


def far_kernel(nodes, value_ref, query_ref, state_ref, decay_ref, residue_ref, far_ref, out_ref):
    decay = decay_ref[...]
    start = residue_ref[...] * state_ref[...]
    node_col = column(nodes + 1.0)
    total = None
    for m in range(decay.shape[0]):
        part = jnp.exp(-node_col * decay[m : m + 1]) * start[m : m + 1]
        total = part if total is None else total + part
    long_conv = value_ref[...] + dot(far_ref[...], tripled(total))
    out_ref[...] = (query_ref[...].astype(F32) * long_conv).astype(BF16)


def per_device(mr_qkv, mr_filter, li_gates, decay, residue):
    rows = mr_qkv.shape[0]
    channels = mr_qkv.shape[1] // 3
    modes = decay.shape[1]
    count, mine = lax.axis_size("ctx"), lax.axis_index("ctx")
    edge = (
        mr_qkv[rows - LEN :, channels : 2 * channels].astype(F32)
        * mr_qkv[rows - LEN :, 2 * channels :].astype(F32)
    ).astype(BF16)
    halo = lax.ppermute(edge, "ctx", [(i - 1, i) for i in range(1, count)])
    decay_rows = decay.T
    residue_rows = residue.T

    width = 256
    tiles = channels // width
    nodes, *consts = tables(width)
    consts = [jnp.asarray(c, BF16) for c in consts]
    whole = lambda c: pl.BlockSpec(c.shape, lambda j: (0, 0))
    part = lambda height, k: pl.BlockSpec((height, width), lambda j, k=k: (0, k * tiles + j))
    values, ended = pl.pallas_call(
        functools.partial(near_kernel, nodes),
        grid=(tiles,),
        in_specs=[
            part(rows, 0), part(rows, 1), part(rows, 2), part(LEN, 0), part(rows, 1),
            pl.BlockSpec((width // 16, LEN), lambda j: (j, 0)),
            part(modes, 0), part(modes, 0),
        ] + [whole(c) for c in consts],
        out_specs=[part(rows, 0), part(modes, 0)],
        out_shape=[
            jax.ShapeDtypeStruct((rows, channels), F32),
            jax.ShapeDtypeStruct((modes, channels), F32),
        ],
        compiler_params=pltpu.CompilerParams(vmem_limit_bytes=48 * 2**20),
        name="near",
    )(mr_qkv, mr_qkv, mr_qkv, halo, li_gates, mr_filter, decay_rows, residue_rows, *consts)

    share = channels // count
    mine_all = lax.all_to_all(
        ended.reshape(modes, count, share), "ctx", split_axis=1, concat_axis=0, tiled=False
    ).reshape(count, modes, share)
    own_decay = jnp.exp(-lax.dynamic_slice_in_dim(decay_rows, mine * share, share, 1) * rows)
    running = jnp.zeros_like(own_decay)
    starts = []
    for k in range(count):
        starts.append(running)
        running = own_decay * running + mine_all[k]
    incoming = lax.all_to_all(
        jnp.stack(starts), "ctx", split_axis=0, concat_axis=1, tiled=False
    ).reshape(modes, channels)

    far_nodes, far_basis = lagrange(rows, FAR_NODES)
    far_high, far_low = halves(far_basis)
    far = jnp.asarray(np.concatenate([far_high, far_low, far_high], axis=1), BF16)
    return pl.pallas_call(
        functools.partial(far_kernel, far_nodes),
        grid=(tiles,),
        in_specs=[
            part(rows, 0), part(rows, 0), part(modes, 0), part(modes, 0), part(modes, 0), whole(far)
        ],
        out_specs=part(rows, 0),
        out_shape=jax.ShapeDtypeStruct((rows, channels), BF16),
        compiler_params=pltpu.CompilerParams(vmem_limit_bytes=48 * 2**20),
        name="far",
    )(values, li_gates, incoming, decay_rows, residue_rows, far)


def solution(mesh):
    return jax.shard_map(
        per_device,
        mesh=mesh,
        in_specs=(P(("groups", "ctx"), None), P(), P(("groups", "ctx"), None), P(), P()),
        out_specs=P(("groups", "ctx"), None),
        check_vma=False,
    )
```

```python
import functools

import jax
import jax.numpy as jnp
import numpy as np
from jax import lax
from jax.experimental import pallas as pl
from jax.experimental.pallas import tpu as pltpu
from jax.sharding import PartitionSpec as P

F32 = jnp.float32
BF16 = jnp.bfloat16
LEN = 128
NODES = 16
FAR_NODES = 32


def halves(table):
    high = table.astype(BF16)
    low = (table - high.astype(np.float64)).astype(BF16)
    return high, low


def lagrange(length, count):
    angle = (2 * np.arange(count) + 1) * np.pi / (2 * count)
    unit = np.cos(angle)
    weight = (-1.0) ** np.arange(count) * np.sin(angle)
    middle = (length - 1) / 2
    points = (np.arange(length) - middle) / middle
    gap = points[:, None] - unit[None, :]
    hit = np.abs(gap) < 1e-14
    ratio = weight[None, :] / np.where(hit, 1.0, gap)
    basis = ratio / ratio.sum(axis=1, keepdims=True)
    rows = hit.any(axis=1)
    basis[rows] = hit[rows]
    return middle + middle * unit, basis


def tables(width):
    freq = np.concatenate([np.arange(0, LEN, 2), np.arange(1, LEN, 2)])
    theta = np.pi * (freq[:, None] + 0.5) * np.arange(LEN)[None, :] / LEN
    forward = np.concatenate([np.cos(theta), -np.sin(theta)], axis=0)
    inverse = (forward.T / LEN).astype(BF16)
    nodes, basis = lagrange(LEN, NODES)
    fwd = np.concatenate([forward, basis[::-1].T], axis=0)
    fwd = np.concatenate(halves(fwd), axis=1)
    tap_high, tap_low = halves(forward @ basis)
    taps = np.concatenate([tap_high, tap_low, tap_high], axis=1)
    near_high, near_low = halves(basis)
    near = np.concatenate([near_high, near_low, near_high], axis=1)
    group = np.arange(width)[None, :] // 16 == np.arange(width // 16)[:, None]
    packed, spans, start = [], [], 0
    for table in (fwd, inverse, near, taps, group):
        table = np.asarray(table, BF16)
        height, depth = table.shape
        spans.append((start, start + height, depth))
        packed.append(np.pad(table, ((0, 0), (0, 2 * LEN - depth))))
        start += height
    return nodes, np.concatenate(packed, axis=0), spans


def table_at(packed_ref, span):
    first, last, depth = span
    return packed_ref[first:last, :depth]


def dot(a, b):
    return lax.dot_general(a, b, (((1,), (0,)), ((), ())), preferred_element_type=F32)


def tripled(values):
    high = values.astype(BF16)
    low = (values - high.astype(F32)).astype(BF16)
    return jnp.concatenate([high, high, low], axis=0)


def twice(values):
    return jnp.concatenate([values, values], axis=0)


def times(re, im, filter_re, filter_im):
    return jnp.concatenate(
        [
            (re * filter_re - im * filter_im).astype(BF16),
            (re * filter_im + im * filter_re).astype(BF16),
        ],
        axis=0,
    )


def column(values):
    rows = lax.broadcasted_iota(jnp.int32, (len(values), 1), 0)
    total = jnp.zeros((len(values), 1), F32)
    for k, value in enumerate(values):
        total = jnp.where(rows == k, np.float32(value), total)
    return total


def weighted(rows_ref, weights):
    total = None
    for m in range(weights.shape[0]):
        part = rows_ref[m * NODES : (m + 1) * NODES, :] * weights[m : m + 1]
        total = part if total is None else total + part
    return total


def prepare_kernel(
    nodes, spans, filt_ref, decay_ref, residue_ref, packed_ref,
    short_ref, long_ref, node_ref, mode_ref,
):
    fwd = table_at(packed_ref, spans[0])[: 2 * LEN]
    decay = decay_ref[...]
    modes = decay.shape[0]
    node_col = column(nodes)
    for m in range(modes):
        node_ref[m * NODES : (m + 1) * NODES, :] = jnp.exp(-node_col * decay[m : m + 1])
    for k, node in enumerate(nodes):
        mode_ref[k * modes : (k + 1) * modes, :] = jnp.exp(-np.float32(node) * decay)
    expanded = lax.dot_general(
        filt_ref[...],
        table_at(packed_ref, spans[4]),
        (((0,), (0,)), ((), ())),
        preferred_element_type=F32,
    ).astype(BF16)
    short_ref[...] = dot(fwd, twice(expanded))
    long_ref[...] = dot(
        table_at(packed_ref, spans[3]), tripled(weighted(node_ref, residue_ref[...]))
    )


def near_kernel(
    spans, q_ref, k_ref, v_ref, halo_ref, key_ref, decay_ref, residue_ref,
    short_ref, long_ref, node_ref, mode_ref, packed_ref, out_ref, sum_ref,
):
    blocks = q_ref.shape[0] // LEN
    half = LEN // 2
    modes = decay_ref.shape[0]
    fwd_all = table_at(packed_ref, spans[0])
    fwd = fwd_all[: 2 * LEN]
    inv = table_at(packed_ref, spans[1])
    near = table_at(packed_ref, spans[2])
    decay = decay_ref[...]
    weight = residue_ref[...] * jnp.exp(-decay)
    step = jnp.exp(-np.float32(LEN) * decay)
    short_re, short_im = short_ref[:LEN, :], short_ref[LEN:, :]
    long_re, long_im = long_ref[:LEN, :], long_ref[LEN:, :]

    before = dot(fwd, twice(halo_ref[...]))
    state = None
    for i in range(blocks):
        rows = pl.ds(i * LEN, LEN)
        product = (k_ref[rows, :].astype(F32) * v_ref[rows, :].astype(F32)).astype(BF16)
        now = dot(fwd, twice(product))
        turned_re = jnp.concatenate(
            [
                now[:half] - before[LEN : LEN + half],
                now[half:LEN] + before[LEN + half :],
            ],
            axis=0,
        )
        turned_im = jnp.concatenate(
            [
                now[LEN : LEN + half] + before[:half],
                now[LEN + half :] - before[half:LEN],
            ],
            axis=0,
        )
        convolved = dot(inv, times(turned_re, turned_im, short_re, short_im))
        before = now
        li_input = key_ref[rows, :].astype(F32) * (q_ref[rows, :].astype(F32) * convolved)
        seen = dot(fwd_all, twice(li_input.astype(BF16)))
        value = dot(inv, times(seen[:LEN], seen[LEN : 2 * LEN], long_re, long_im))
        if state is not None:
            value = value + dot(near, tripled(weighted(node_ref, weight * state)))
        out_ref[rows, :] = value
        ended = None
        for k in range(NODES):
            part = mode_ref[k * modes : (k + 1) * modes, :] * seen[2 * LEN + k : 2 * LEN + k + 1]
            ended = part if ended is None else ended + part
        state = ended if state is None else step * state + ended
    sum_ref[...] = state


def exchange_kernel(
    count, tokens, ended_ref, decay_ref, out_ref, got, starts, landed,
    send_one, recv_one, send_two, recv_two,
):
    mine = lax.axis_index("ctx")
    share = got.shape[2]

    def other(k):
        return lax.rem(mine + k, count)

    def columns(k):
        return pl.ds(pl.multiple_of(k * share, share), share)

    def first(k):
        return pltpu.make_async_remote_copy(
            src_ref=ended_ref.at[:, columns(k)],
            dst_ref=got.at[mine],
            send_sem=send_one.at[k],
            recv_sem=recv_one.at[mine],
            device_id={"ctx": k},
            device_id_type=pl.DeviceIdType.MESH,
        )

    def arrived(buffer, sem, k):
        return pltpu.make_async_remote_copy(
            src_ref=buffer.at[k],
            dst_ref=buffer.at[k],
            send_sem=sem.at[k],
            recv_sem=sem.at[k],
            device_id={"ctx": k},
            device_id_type=pl.DeviceIdType.MESH,
        )

    def second(k):
        return pltpu.make_async_remote_copy(
            src_ref=starts.at[k],
            dst_ref=landed.at[mine],
            send_sem=send_two.at[k],
            recv_sem=recv_two.at[mine],
            device_id={"ctx": k},
            device_id_type=pl.DeviceIdType.MESH,
        )

    barrier = pltpu.get_barrier_semaphore()

    @pl.loop(1, count)
    def _(k):
        pl.semaphore_signal(
            barrier, inc=1, device_id={"ctx": other(k)}, device_id_type=pl.DeviceIdType.MESH
        )

    pl.semaphore_wait(barrier, count - 1)

    @pl.loop(1, count)
    def _(k):
        first(other(k)).start()

    got[mine] = ended_ref[:, columns(mine)]
    own_decay = jnp.exp(-np.float32(tokens) * decay_ref[:, columns(mine)])

    def turn(k, running):
        starts[k] = running

        @pl.when(k != mine)
        def _():
            second(k).start()
            arrived(got, recv_one, k).wait_recv()

        return own_decay * running + got[k]

    lax.fori_loop(0, count, turn, jnp.zeros(own_decay.shape, F32))
    landed[mine] = starts[mine]

    @pl.loop(1, count)
    def _(k):
        arrived(landed, recv_two, other(k)).wait_recv()

    @pl.loop(0, count)
    def _(k):
        out_ref[:, columns(k)] = landed[k]

    @pl.loop(1, count)
    def _(k):
        first(other(k)).wait_send()
        second(other(k)).wait_send()


def far_kernel(nodes, value_ref, query_ref, state_ref, decay_ref, residue_ref, far_ref, out_ref):
    decay = decay_ref[...]
    start = residue_ref[...] * state_ref[...]
    node_col = column(nodes + 1.0)
    total = None
    for m in range(decay.shape[0]):
        part = jnp.exp(-node_col * decay[m : m + 1]) * start[m : m + 1]
        total = part if total is None else total + part
    long_conv = value_ref[...] + dot(far_ref[...], tripled(total))
    out_ref[...] = (query_ref[...].astype(F32) * long_conv).astype(BF16)


def per_device(mr_qkv, mr_filter, li_gates, decay, residue):
    rows = mr_qkv.shape[0]
    channels = mr_qkv.shape[1] // 3
    modes = decay.shape[1]
    count = lax.axis_size("ctx")
    edge = (
        mr_qkv[rows - LEN :, channels : 2 * channels].astype(F32)
        * mr_qkv[rows - LEN :, 2 * channels :].astype(F32)
    ).astype(BF16)
    halo = lax.ppermute(edge, "ctx", [(i - 1, i) for i in range(1, count)])
    decay_rows = decay.T
    residue_rows = residue.T

    width = 256
    tiles = channels // width
    nodes, packed, spans = tables(width)
    packed = jnp.asarray(packed)
    whole = lambda c: pl.BlockSpec(c.shape, lambda j: (0, 0))
    part = lambda height, k=0: pl.BlockSpec((height, width), lambda j, k=k: (0, k * tiles + j))
    shape = lambda height: jax.ShapeDtypeStruct((height, channels), F32)
    params = pltpu.CompilerParams(vmem_limit_bytes=48 * 2**20)
    heights = (2 * LEN, 2 * LEN, modes * NODES, modes * NODES)
    prepared = pl.pallas_call(
        functools.partial(prepare_kernel, nodes, spans),
        grid=(tiles,),
        in_specs=[
            pl.BlockSpec((width // 16, LEN), lambda j: (j, 0)),
            part(modes), part(modes), whole(packed),
        ],
        out_specs=[part(height) for height in heights],
        out_shape=[shape(height) for height in heights],
        compiler_params=params,
        name="prepare",
    )(mr_filter, decay_rows, residue_rows, packed)
    values, ended = pl.pallas_call(
        functools.partial(near_kernel, spans),
        grid=(tiles,),
        in_specs=[
            part(rows, 0), part(rows, 1), part(rows, 2), part(LEN), part(rows, 1),
            part(modes), part(modes),
        ] + [part(height) for height in heights] + [whole(packed)],
        out_specs=[part(rows), part(modes)],
        out_shape=[shape(rows), shape(modes)],
        compiler_params=params,
        name="near",
    )(mr_qkv, mr_qkv, mr_qkv, halo, li_gates, decay_rows, residue_rows, *prepared, packed)

    share = channels // count
    slots = pltpu.VMEM((count, modes, share), F32)
    incoming = pl.pallas_call(
        functools.partial(exchange_kernel, count, rows),
        in_specs=[pl.BlockSpec(memory_space=pltpu.VMEM)] * 2,
        out_specs=pl.BlockSpec(memory_space=pltpu.VMEM),
        out_shape=shape(modes),
        scratch_shapes=[slots] * 3 + [pltpu.SemaphoreType.DMA((count,))] * 4,
        compiler_params=pltpu.CompilerParams(collective_id=0, has_side_effects=True),
        name="exchange",
    )(ended, decay_rows)

    far_nodes, far_basis = lagrange(rows, FAR_NODES)
    far_high, far_low = halves(far_basis)
    far = jnp.asarray(np.concatenate([far_high, far_low, far_high], axis=1), BF16)
    return pl.pallas_call(
        functools.partial(far_kernel, far_nodes),
        grid=(tiles,),
        in_specs=[
            part(rows), part(rows), part(modes), part(modes), part(modes), whole(far)
        ],
        out_specs=part(rows),
        out_shape=jax.ShapeDtypeStruct((rows, channels), BF16),
        compiler_params=pltpu.CompilerParams(vmem_limit_bytes=48 * 2**20),
        name="far",
    )(values, li_gates, incoming, decay_rows, residue_rows, far)


def solution(mesh):
    return jax.shard_map(
        per_device,
        mesh=mesh,
        in_specs=(P(("groups", "ctx"), None), P(), P(("groups", "ctx"), None), P(), P()),
        out_specs=P(("groups", "ctx"), None),
        check_vma=False,
    )
```

```python
import functools

import jax
import jax.numpy as jnp
import numpy as np
from jax import lax
from jax.experimental import pallas as pl
from jax.experimental.pallas import tpu as pltpu
from jax.sharding import PartitionSpec as P

F32 = jnp.float32
BF16 = jnp.bfloat16
LEN = 128
NODES = 16
CHUNK = 256


def halves(table):
    high = table.astype(BF16)
    low = (table - high.astype(np.float64)).astype(BF16)
    return high, low


def lagrange(length, count):
    angle = (2 * np.arange(count) + 1) * np.pi / (2 * count)
    unit = np.cos(angle)
    weight = (-1.0) ** np.arange(count) * np.sin(angle)
    middle = (length - 1) / 2
    points = (np.arange(length) - middle) / middle
    gap = points[:, None] - unit[None, :]
    hit = np.abs(gap) < 1e-14
    ratio = weight[None, :] / np.where(hit, 1.0, gap)
    basis = ratio / ratio.sum(axis=1, keepdims=True)
    rows = hit.any(axis=1)
    basis[rows] = hit[rows]
    return middle + middle * unit, basis


def tables(width):
    freq = np.concatenate([np.arange(0, LEN, 2), np.arange(1, LEN, 2)])
    theta = np.pi * (freq[:, None] + 0.5) * np.arange(LEN)[None, :] / LEN
    forward = np.concatenate([np.cos(theta), -np.sin(theta)], axis=0)
    inverse = (forward.T / LEN).astype(BF16)
    nodes, basis = lagrange(LEN, NODES)
    fwd = np.concatenate([forward, basis[::-1].T], axis=0)
    fwd = np.concatenate(halves(fwd), axis=1)
    tap_high, tap_low = halves(forward @ basis)
    taps = np.concatenate([tap_high, tap_low, tap_high], axis=1)
    near_high, near_low = halves(basis)
    near = np.concatenate([near_high, near_low, near_high], axis=1)
    group = np.arange(width)[None, :] // 16 == np.arange(width // 16)[:, None]
    packed, spans, start = [], [], 0
    for table in (fwd, inverse, near, taps, group):
        table = np.asarray(table, BF16)
        height, depth = table.shape
        spans.append((start, start + height, depth))
        packed.append(np.pad(table, ((0, 0), (0, 2 * LEN - depth))))
        start += height
    return nodes, np.concatenate(packed, axis=0), spans


def table_at(packed_ref, span):
    first, last, depth = span
    return packed_ref[first:last, :depth]


def dot(a, b):
    return lax.dot_general(a, b, (((1,), (0,)), ((), ())), preferred_element_type=F32)


def tripled(values):
    high = values.astype(BF16)
    low = (values - high.astype(F32)).astype(BF16)
    return jnp.concatenate([high, high, low], axis=0)


def twice(values):
    return jnp.concatenate([values, values], axis=0)


def times(re, im, filter_re, filter_im):
    return jnp.concatenate(
        [
            (re * filter_re - im * filter_im).astype(BF16),
            (re * filter_im + im * filter_re).astype(BF16),
        ],
        axis=0,
    )


def column(values):
    rows = lax.broadcasted_iota(jnp.int32, (len(values), 1), 0)
    total = jnp.zeros((len(values), 1), F32)
    for k, value in enumerate(values):
        total = jnp.where(rows == k, np.float32(value), total)
    return total


def weighted(rows_ref, base, weights):
    total = None
    for m in range(weights.shape[0]):
        first = base + m * NODES
        part = rows_ref[first : first + NODES, :] * weights[m : m + 1]
        total = part if total is None else total + part
    return total


def prepare_kernel(nodes, spans, filt_ref, modal_ref, packed_ref, out_ref):
    fwd = table_at(packed_ref, spans[0])[: 2 * LEN]
    modes = modal_ref.shape[0] // 2
    decay = modal_ref[:modes, :]
    residue = modal_ref[modes:, :]
    node_col = column(nodes)
    base = 4 * LEN
    end = base + modes * NODES
    for m in range(modes):
        out_ref[base + m * NODES : base + (m + 1) * NODES, :] = jnp.exp(-node_col * decay[m : m + 1])
    for k, node in enumerate(nodes):
        out_ref[end + k * modes : end + (k + 1) * modes, :] = jnp.exp(-np.float32(node) * decay)
    filters = CHUNK // 16
    expanded = jnp.concatenate(
        [
            lax.dot_general(
                filt_ref[i * filters : (i + 1) * filters, :],
                table_at(packed_ref, spans[4]),
                (((0,), (0,)), ((), ())),
                preferred_element_type=F32,
            ).astype(BF16)
            for i in range(decay.shape[1] // CHUNK)
        ],
        axis=1,
    )
    out_ref[: 2 * LEN, :] = dot(fwd, twice(expanded))
    out_ref[2 * LEN : 4 * LEN, :] = dot(
        table_at(packed_ref, spans[3]), tripled(weighted(out_ref, base, residue))
    )


def near_chunk(
    spans, q_ref, k_ref, v_ref, halo_ref, key_ref, modal_ref, prepared_ref, packed_ref,
    out_ref, sum_ref,
):
    blocks = q_ref.shape[0] // LEN
    half = LEN // 2
    modes = modal_ref.shape[0] // 2
    fwd_all = table_at(packed_ref, spans[0])
    fwd = fwd_all[: 2 * LEN]
    inv = table_at(packed_ref, spans[1])
    near = table_at(packed_ref, spans[2])
    base = 4 * LEN
    end = base + modes * NODES
    decay = modal_ref[:modes, :]
    weight = modal_ref[modes:, :] * jnp.exp(-decay)
    step = jnp.exp(-np.float32(LEN) * decay)
    spectra = [dot(fwd, twice(halo_ref[...]))]
    for i in range(blocks):
        rows = pl.ds(i * LEN, LEN)
        product = (k_ref[rows, :].astype(F32) * v_ref[rows, :].astype(F32)).astype(BF16)
        spectra.append(dot(fwd, twice(product)))
    convolved = []
    for before, now in zip(spectra[:-1], spectra[1:]):
        turned_re = jnp.concatenate(
            [
                now[:half] - before[LEN : LEN + half],
                now[half:LEN] + before[LEN + half :],
            ],
            axis=0,
        )
        turned_im = jnp.concatenate(
            [
                now[LEN : LEN + half] + before[:half],
                now[LEN + half :] - before[half:LEN],
            ],
            axis=0,
        )
        short_re, short_im = prepared_ref[:LEN, :], prepared_ref[LEN : 2 * LEN, :]
        convolved.append(dot(inv, times(turned_re, turned_im, short_re, short_im)))
    seen = []
    for i in range(blocks):
        rows = pl.ds(i * LEN, LEN)
        li_input = key_ref[rows, :].astype(F32) * (q_ref[rows, :].astype(F32) * convolved[i])
        seen.append(dot(fwd_all, twice(li_input.astype(BF16))))
    state = None
    for i in range(blocks):
        rows = pl.ds(i * LEN, LEN)
        long_re = prepared_ref[2 * LEN : 3 * LEN, :]
        long_im = prepared_ref[3 * LEN : 4 * LEN, :]
        value = dot(inv, times(seen[i][:LEN], seen[i][LEN : 2 * LEN], long_re, long_im))
        if state is not None:
            value = value + dot(near, tripled(weighted(prepared_ref, base, weight * state)))
        out_ref[rows, :] = value
        ended = None
        for k in range(NODES):
            first = end + k * modes
            weights = prepared_ref[first : first + modes, :]
            part = weights * seen[i][2 * LEN + k : 2 * LEN + k + 1]
            ended = part if ended is None else ended + part
        state = ended if state is None else step * state + ended
    sum_ref[...] = state


def near_kernel(spans, *refs):
    packed_ref = refs[7]
    for i in range(refs[0].shape[1] // CHUNK):
        cut = lambda ref: ref.at[:, i * CHUNK : (i + 1) * CHUNK]
        parts = [ref if ref is packed_ref else cut(ref) for ref in refs]
        near_chunk(spans, *parts)


def far_kernel(spans, value_ref, query_ref, state_ref, modal_ref, node_ref, packed_ref, out_ref):
    modes = modal_ref.shape[0] // 2
    decay = modal_ref[:modes, :]
    near = table_at(packed_ref, spans[2])
    step = jnp.exp(-np.float32(LEN) * decay)
    start = modal_ref[modes:, :] * jnp.exp(-decay) * state_ref[...]
    for i in range(value_ref.shape[0] // LEN):
        rows = pl.ds(i * LEN, LEN)
        long_conv = value_ref[rows, :] + dot(near, tripled(weighted(node_ref, 0, start)))
        out_ref[rows, :] = (query_ref[rows, :].astype(F32) * long_conv).astype(BF16)
        start = step * start


def exchange_kernel(
    count, tokens, ended_ref, decay_ref, out_ref, got, starts, landed,
    send_one, recv_one, send_two, recv_two,
):
    mine = lax.axis_index("ctx")
    share = got.shape[2]

    def other(k):
        return lax.rem(mine + k, count)

    def columns(k):
        return pl.ds(pl.multiple_of(k * share, share), share)

    def first(k):
        return pltpu.make_async_remote_copy(
            src_ref=ended_ref.at[:, columns(k)],
            dst_ref=got.at[mine],
            send_sem=send_one.at[k],
            recv_sem=recv_one.at[mine],
            device_id={"ctx": k},
            device_id_type=pl.DeviceIdType.MESH,
        )

    def arrived(buffer, sem, k):
        return pltpu.make_async_remote_copy(
            src_ref=buffer.at[k],
            dst_ref=buffer.at[k],
            send_sem=sem.at[k],
            recv_sem=sem.at[k],
            device_id={"ctx": k},
            device_id_type=pl.DeviceIdType.MESH,
        )

    def second(k):
        return pltpu.make_async_remote_copy(
            src_ref=starts.at[k],
            dst_ref=landed.at[mine],
            send_sem=send_two.at[k],
            recv_sem=recv_two.at[mine],
            device_id={"ctx": k},
            device_id_type=pl.DeviceIdType.MESH,
        )

    barrier = pltpu.get_barrier_semaphore()

    @pl.loop(1, count)
    def _(k):
        pl.semaphore_signal(
            barrier, inc=1, device_id={"ctx": other(k)}, device_id_type=pl.DeviceIdType.MESH
        )

    pl.semaphore_wait(barrier, count - 1)

    @pl.loop(1, count)
    def _(k):
        first(other(k)).start()

    got[mine] = ended_ref[:, columns(mine)]
    own_decay = jnp.exp(-np.float32(tokens) * decay_ref[: got.shape[1], columns(mine)])

    def turn(k, running):
        starts[k] = running

        @pl.when(k != mine)
        def _():
            second(k).start()
            arrived(got, recv_one, k).wait_recv()

        return own_decay * running + got[k]

    lax.fori_loop(0, count, turn, jnp.zeros(own_decay.shape, F32))
    landed[mine] = starts[mine]

    @pl.loop(1, count)
    def _(k):
        arrived(landed, recv_two, other(k)).wait_recv()

    @pl.loop(0, count)
    def _(k):
        out_ref[:, columns(k)] = landed[k]

    @pl.loop(1, count)
    def _(k):
        first(other(k)).wait_send()
        second(other(k)).wait_send()


def per_device(mr_qkv, mr_filter, li_gates, decay, residue):
    rows = mr_qkv.shape[0]
    channels = mr_qkv.shape[1] // 3
    modes = decay.shape[1]
    count = lax.axis_size("ctx")
    edge = (
        mr_qkv[rows - LEN :, channels : 2 * channels].astype(F32)
        * mr_qkv[rows - LEN :, 2 * channels :].astype(F32)
    ).astype(BF16)
    halo = lax.ppermute(edge, "ctx", [(i - 1, i) for i in range(1, count)])
    modal = jnp.concatenate([decay.T, residue.T], axis=0)

    width = 512
    tiles = channels // width
    nodes, packed, spans = tables(CHUNK)
    packed = jnp.asarray(packed)
    whole = lambda c: pl.BlockSpec(c.shape, lambda j: (0, 0))
    part = lambda height, k=0: pl.BlockSpec((height, width), lambda j, k=k: (0, k * tiles + j))
    shape = lambda height: jax.ShapeDtypeStruct((height, channels), F32)
    params = pltpu.CompilerParams(vmem_limit_bytes=48 * 2**20)
    height = 4 * LEN + 2 * modes * NODES
    prepared = pl.pallas_call(
        functools.partial(prepare_kernel, nodes, spans),
        grid=(tiles,),
        in_specs=[
            pl.BlockSpec((width // 16, LEN), lambda j: (j, 0)), part(2 * modes), whole(packed)
        ],
        out_specs=part(height),
        out_shape=shape(height),
        compiler_params=params,
        name="prepare",
    )(mr_filter, modal, packed)
    values, ended = pl.pallas_call(
        functools.partial(near_kernel, spans),
        grid=(tiles,),
        in_specs=[
            part(rows, 0), part(rows, 1), part(rows, 2), part(LEN), part(rows, 1),
            part(2 * modes), part(height), whole(packed),
        ],
        out_specs=[part(rows), part(modes)],
        out_shape=[shape(rows), shape(modes)],
        compiler_params=params,
        name="near",
    )(mr_qkv, mr_qkv, mr_qkv, halo, li_gates, modal, prepared, packed)

    share = channels // count
    slots = pltpu.VMEM((count, modes, share), F32)
    incoming = pl.pallas_call(
        functools.partial(exchange_kernel, count, rows),
        in_specs=[pl.BlockSpec(memory_space=pltpu.VMEM)] * 2,
        out_specs=pl.BlockSpec(memory_space=pltpu.VMEM),
        out_shape=shape(modes),
        scratch_shapes=[slots] * 3 + [pltpu.SemaphoreType.DMA((count,))] * 4,
        compiler_params=pltpu.CompilerParams(collective_id=0, has_side_effects=True),
        name="exchange",
    )(ended, modal)

    node_part = pl.BlockSpec(
        (modes * NODES, width), lambda j: (4 * LEN // (modes * NODES), j)
    )
    return pl.pallas_call(
        functools.partial(far_kernel, spans),
        grid=(tiles,),
        in_specs=[
            part(rows), part(rows), part(modes), part(2 * modes), node_part, whole(packed)
        ],
        out_specs=part(rows),
        out_shape=jax.ShapeDtypeStruct((rows, channels), BF16),
        compiler_params=params,
        name="far",
    )(values, li_gates, incoming, modal, prepared, packed)


def solution(mesh):
    return jax.shard_map(
        per_device,
        mesh=mesh,
        in_specs=(P(("groups", "ctx"), None), P(), P(("groups", "ctx"), None), P(), P()),
        out_specs=P(("groups", "ctx"), None),
        check_vma=False,
    )
```

```python
import functools

import jax
import jax.numpy as jnp
import numpy as np
from jax import lax
from jax.experimental import pallas as pl
from jax.experimental.pallas import tpu as pltpu
from jax.sharding import PartitionSpec as P

F32 = jnp.float32
BF16 = jnp.bfloat16
LEN = 128
NODES = 16
CHUNK = 256


def halves(table):
    high = table.astype(BF16)
    low = (table - high.astype(np.float64)).astype(BF16)
    return high, low


def lagrange(length, count):
    angle = (2 * np.arange(count) + 1) * np.pi / (2 * count)
    unit = np.cos(angle)
    weight = (-1.0) ** np.arange(count) * np.sin(angle)
    middle = (length - 1) / 2
    points = (np.arange(length) - middle) / middle
    gap = points[:, None] - unit[None, :]
    hit = np.abs(gap) < 1e-14
    ratio = weight[None, :] / np.where(hit, 1.0, gap)
    basis = ratio / ratio.sum(axis=1, keepdims=True)
    rows = hit.any(axis=1)
    basis[rows] = hit[rows]
    return middle + middle * unit, basis


def tables(width):
    freq = np.concatenate([np.arange(0, LEN, 2), np.arange(1, LEN, 2)])
    theta = np.pi * (freq[:, None] + 0.5) * np.arange(LEN)[None, :] / LEN
    forward = np.concatenate([np.cos(theta), -np.sin(theta)], axis=0)
    inverse = (forward.T / LEN).astype(BF16)
    nodes, basis = lagrange(LEN, NODES)
    fwd = np.concatenate([forward, basis[::-1].T], axis=0)
    fwd = np.concatenate(halves(fwd), axis=1)
    tap_high, tap_low = halves(forward @ basis)
    taps = np.concatenate([tap_high, tap_low, tap_high], axis=1)
    near_high, near_low = halves(basis)
    near = np.concatenate([near_high, near_low, near_high], axis=1)
    group = np.arange(width)[None, :] // 16 == np.arange(width // 16)[:, None]
    packed, spans, start = [], [], 0
    for table in (fwd, inverse, near, taps, group):
        table = np.asarray(table, BF16)
        height, depth = table.shape
        spans.append((start, start + height, depth))
        packed.append(np.pad(table, ((0, 0), (0, 2 * LEN - depth))))
        start += height
    return nodes, np.concatenate(packed, axis=0), spans


def table_at(packed_ref, span):
    first, last, depth = span
    return packed_ref[first:last, :depth]


def dot(a, b):
    return lax.dot_general(a, b, (((1,), (0,)), ((), ())), preferred_element_type=F32)


def tripled(values):
    high = values.astype(BF16)
    low = (values - high.astype(F32)).astype(BF16)
    return jnp.concatenate([high, high, low], axis=0)


def twice(values):
    return jnp.concatenate([values, values], axis=0)


def times(re, im, filter_re, filter_im):
    return jnp.concatenate(
        [
            (re * filter_re - im * filter_im).astype(BF16),
            (re * filter_im + im * filter_re).astype(BF16),
        ],
        axis=0,
    )


def column(values):
    rows = lax.broadcasted_iota(jnp.int32, (len(values), 1), 0)
    total = jnp.zeros((len(values), 1), F32)
    for k, value in enumerate(values):
        total = jnp.where(rows == k, np.float32(value), total)
    return total


def weighted(rows_ref, base, weights):
    total = None
    for m in range(weights.shape[0]):
        first = base + m * NODES
        part = rows_ref[first : first + NODES, :] * weights[m : m + 1]
        total = part if total is None else total + part
    return total


def prepare_kernel(nodes, spans, filt_ref, modal_ref, packed_ref, out_ref):
    fwd = table_at(packed_ref, spans[0])[: 2 * LEN]
    modes = modal_ref.shape[0] // 2
    decay = modal_ref[:modes, :]
    residue = modal_ref[modes:, :]
    node_col = column(nodes)
    base = 4 * LEN
    end = base + modes * NODES
    for m in range(modes):
        out_ref[base + m * NODES : base + (m + 1) * NODES, :] = jnp.exp(-node_col * decay[m : m + 1])
    for k, node in enumerate(nodes):
        out_ref[end + k * modes : end + (k + 1) * modes, :] = jnp.exp(-np.float32(node) * decay)
    filters = CHUNK // 16
    expanded = jnp.concatenate(
        [
            lax.dot_general(
                filt_ref[i * filters : (i + 1) * filters, :],
                table_at(packed_ref, spans[4]),
                (((0,), (0,)), ((), ())),
                preferred_element_type=F32,
            ).astype(BF16)
            for i in range(decay.shape[1] // CHUNK)
        ],
        axis=1,
    )
    out_ref[: 2 * LEN, :] = dot(fwd, twice(expanded))
    out_ref[2 * LEN : 4 * LEN, :] = dot(
        table_at(packed_ref, spans[3]), tripled(weighted(out_ref, base, residue))
    )


def near_chunk(
    spans, q_ref, k_ref, v_ref, halo_ref, key_ref, modal_ref, prepared_ref, packed_ref,
    out_ref,
):
    blocks = q_ref.shape[0] // LEN
    half = LEN // 2
    modes = modal_ref.shape[0] // 2
    fwd_all = table_at(packed_ref, spans[0])
    fwd = fwd_all[: 2 * LEN]
    inv = table_at(packed_ref, spans[1])
    near = table_at(packed_ref, spans[2])
    base = 4 * LEN
    end = base + modes * NODES
    decay = modal_ref[:modes, :]
    weight = modal_ref[modes:, :] * jnp.exp(-decay)
    step = jnp.exp(-np.float32(LEN) * decay)
    spectra = [dot(fwd, twice(halo_ref[...]))]
    for i in range(blocks):
        rows = pl.ds(i * LEN, LEN)
        product = (k_ref[rows, :].astype(F32) * v_ref[rows, :].astype(F32)).astype(BF16)
        spectra.append(dot(fwd, twice(product)))
    convolved = []
    for before, now in zip(spectra[:-1], spectra[1:]):
        turned_re = jnp.concatenate(
            [
                now[:half] - before[LEN : LEN + half],
                now[half:LEN] + before[LEN + half :],
            ],
            axis=0,
        )
        turned_im = jnp.concatenate(
            [
                now[LEN : LEN + half] + before[:half],
                now[LEN + half :] - before[half:LEN],
            ],
            axis=0,
        )
        short_re, short_im = prepared_ref[:LEN, :], prepared_ref[LEN : 2 * LEN, :]
        convolved.append(dot(inv, times(turned_re, turned_im, short_re, short_im)))
    seen = []
    for i in range(blocks):
        rows = pl.ds(i * LEN, LEN)
        li_input = key_ref[rows, :].astype(F32) * (q_ref[rows, :].astype(F32) * convolved[i])
        seen.append(dot(fwd_all, twice(li_input.astype(BF16))))
    state = None
    for i in range(blocks):
        rows = pl.ds(i * LEN, LEN)
        long_re = prepared_ref[2 * LEN : 3 * LEN, :]
        long_im = prepared_ref[3 * LEN : 4 * LEN, :]
        value = dot(inv, times(seen[i][:LEN], seen[i][LEN : 2 * LEN], long_re, long_im))
        if state is not None:
            value = value + dot(near, tripled(weighted(prepared_ref, base, weight * state)))
        out_ref[rows, :] = value
        ended = None
        for k in range(NODES):
            first = end + k * modes
            weights = prepared_ref[first : first + modes, :]
            part = weights * seen[i][2 * LEN + k : 2 * LEN + k + 1]
            ended = part if ended is None else ended + part
        state = ended if state is None else step * state + ended
    return state


def far_tile(spans, value_ref, query_ref, state, modal_ref, node_ref, packed_ref, out_ref):
    modes = modal_ref.shape[0] // 2
    decay = modal_ref[:modes, :]
    near = table_at(packed_ref, spans[2])
    step = jnp.exp(-np.float32(LEN) * decay)
    start = modal_ref[modes:, :] * jnp.exp(-decay) * state
    for i in range(query_ref.shape[0] // LEN):
        rows = pl.ds(i * LEN, LEN)
        long_conv = value_ref[rows, :] + dot(near, tripled(weighted(node_ref, 0, start)))
        out_ref[rows, :] = (query_ref[rows, :].astype(F32) * long_conv).astype(BF16)
        start = step * start


def main_kernel(
    spans, count, tiles, q_ref, k_ref, v_ref, halo_ref, key_ref, modal_ref, prepared_ref,
    packed_ref, all_ref, query_ref, node_ref, out_ref, values, ended, got, starts, landed,
    send_one, recv_one, send_two, recv_two,
):
    turn_now = pl.program_id(0)
    mine = lax.axis_index("ctx")
    tokens, width = q_ref.shape
    modes, share = got.shape[1:]
    per = width // share

    def copy(source, target, send, recv, slot, k):
        return pltpu.make_async_remote_copy(
            src_ref=source.at[k],
            dst_ref=target.at[slot],
            send_sem=send.at[k],
            recv_sem=recv.at[slot],
            device_id={"ctx": k},
            device_id_type=pl.DeviceIdType.MESH,
        )

    def first(k):
        return copy(ended, got, send_one, recv_one, mine, k)

    def second(k):
        return copy(starts, landed, send_two, recv_two, mine, k)

    def arrived(buffer, sem, k):
        return copy(buffer, buffer, sem, sem, k, k)

    def other(k):
        return lax.rem(mine + k, count)

    @pl.when(turn_now == 0)
    def _():
        barrier = pltpu.get_barrier_semaphore()

        @pl.loop(1, count)
        def _(k):
            pl.semaphore_signal(
                barrier, inc=1, device_id={"ctx": other(k)}, device_id_type=pl.DeviceIdType.MESH
            )

        pl.semaphore_wait(barrier, count - 1)

    @pl.when(turn_now < tiles)
    def _():
        refs = [q_ref, k_ref, v_ref, halo_ref, key_ref, modal_ref, prepared_ref]
        states = []
        for i in range(width // CHUNK):
            columns = slice(i * CHUNK, (i + 1) * CHUNK)
            parts = [ref.at[:, columns] for ref in refs]
            states.append(
                near_chunk(spans, *parts, packed_ref, values.at[turn_now, :, columns])
            )
        state = jnp.concatenate(states, axis=1)
        for i in range(per):
            owner = turn_now * per + i
            ended[owner] = state[:, i * share : (i + 1) * share]

            @pl.when(owner != mine)
            def _():
                first(owner).start()

    last = tiles - 1
    own = lax.div(mine, per)

    @pl.when((turn_now == own + 1) & (own < last) | (turn_now == last) & (own == last))
    def _():
        columns = pl.ds(pl.multiple_of(mine * share, share), share)
        own_decay = jnp.exp(-np.float32(tokens) * all_ref[:modes, columns])
        got[mine] = ended[mine]

        def turn(k, running):
            starts[k] = running

            @pl.when(k != mine)
            def _():
                second(k).start()
                arrived(got, recv_one, k).wait_recv()

            return own_decay * running + got[k]

        lax.fori_loop(0, count, turn, jnp.zeros((modes, share), F32))
        landed[mine] = starts[mine]

    @pl.when(turn_now >= tiles)
    def _():
        tile = turn_now - tiles
        for i in range(per):
            owner = tile * per + i

            @pl.when(owner != mine)
            def _():
                arrived(landed, recv_two, owner).wait_recv()

        state = jnp.concatenate([landed[tile * per + i] for i in range(per)], axis=1)
        far_tile(
            spans, values.at[tile], query_ref, state, modal_ref, node_ref, packed_ref, out_ref
        )

    @pl.when(turn_now == 2 * tiles - 1)
    def _():
        @pl.loop(1, count)
        def _(k):
            first(other(k)).wait_send()
            second(other(k)).wait_send()


def per_device(mr_qkv, mr_filter, li_gates, decay, residue):
    rows = mr_qkv.shape[0]
    channels = mr_qkv.shape[1] // 3
    modes = decay.shape[1]
    count = lax.axis_size("ctx")
    edge = (
        mr_qkv[rows - LEN :, channels : 2 * channels].astype(F32)
        * mr_qkv[rows - LEN :, 2 * channels :].astype(F32)
    ).astype(BF16)
    halo = lax.ppermute(edge, "ctx", [(i - 1, i) for i in range(1, count)])
    modal = jnp.concatenate([decay.T, residue.T], axis=0)

    width = 512
    tiles = channels // width
    nodes, packed, spans = tables(CHUNK)
    packed = jnp.asarray(packed)
    whole = lambda c: pl.BlockSpec(c.shape, lambda j: (0, 0))
    part = lambda height, k=0: pl.BlockSpec((height, width), lambda j, k=k: (0, k * tiles + j))
    shape = lambda height: jax.ShapeDtypeStruct((height, channels), F32)
    params = pltpu.CompilerParams(vmem_limit_bytes=48 * 2**20)
    height = 4 * LEN + 2 * modes * NODES
    prepared = pl.pallas_call(
        functools.partial(prepare_kernel, nodes, spans),
        grid=(tiles,),
        in_specs=[
            pl.BlockSpec((width // 16, LEN), lambda j: (j, 0)), part(2 * modes), whole(packed)
        ],
        out_specs=part(height),
        out_shape=shape(height),
        compiler_params=params,
        name="prepare",
    )(mr_filter, modal, packed)
    def held(height, k=0):
        def place(j):
            return 0, k * tiles + j - lax.div(j, tiles) * (j - tiles + 1)

        return pl.BlockSpec((height, width), place)

    def later(height, k=0):
        return pl.BlockSpec((height, width), lambda j: (k, lax.div(j, tiles) * (j - tiles)))

    share = channels // count
    slots = pltpu.VMEM((count, modes, share), F32)
    return pl.pallas_call(
        functools.partial(main_kernel, spans, count, tiles),
        grid=(2 * tiles,),
        in_specs=[
            held(rows, 0), held(rows, 1), held(rows, 2), held(LEN), held(rows, 1),
            pl.BlockSpec((2 * modes, width), lambda j: (0, lax.rem(j, tiles))),
            held(height), whole(packed), whole(modal), later(rows),
            later(modes * NODES, 4 * LEN // (modes * NODES)),
        ],
        out_specs=later(rows),
        out_shape=jax.ShapeDtypeStruct((rows, channels), BF16),
        scratch_shapes=[pltpu.VMEM((tiles, rows, width), F32)]
        + [slots] * 4
        + [pltpu.SemaphoreType.DMA((count,))] * 4,
        compiler_params=pltpu.CompilerParams(
            vmem_limit_bytes=52 * 2**20, collective_id=0, has_side_effects=True
        ),
        name="main",
    )(
        mr_qkv, mr_qkv, mr_qkv, halo, li_gates, modal, prepared, packed, modal, li_gates, prepared
    )


def solution(mesh):
    return jax.shard_map(
        per_device,
        mesh=mesh,
        in_specs=(P(("groups", "ctx"), None), P(), P(("groups", "ctx"), None), P(), P()),
        out_specs=P(("groups", "ctx"), None),
        check_vma=False,
    )
```

```python
import functools

import jax
import jax.numpy as jnp
import numpy as np
from jax import lax
from jax.experimental import pallas as pl
from jax.experimental.pallas import tpu as pltpu
from jax.sharding import PartitionSpec as P

F32 = jnp.float32
BF16 = jnp.bfloat16
LEN = 128
NODES = 16
CHUNK = 256


def halves(table):
    high = table.astype(BF16)
    low = (table - high.astype(np.float64)).astype(BF16)
    return high, low


def lagrange(length, count):
    angle = (2 * np.arange(count) + 1) * np.pi / (2 * count)
    unit = np.cos(angle)
    weight = (-1.0) ** np.arange(count) * np.sin(angle)
    middle = (length - 1) / 2
    points = (np.arange(length) - middle) / middle
    gap = points[:, None] - unit[None, :]
    hit = np.abs(gap) < 1e-14
    ratio = weight[None, :] / np.where(hit, 1.0, gap)
    basis = ratio / ratio.sum(axis=1, keepdims=True)
    rows = hit.any(axis=1)
    basis[rows] = hit[rows]
    return middle + middle * unit, basis


def tables(width):
    freq = np.concatenate([np.arange(0, LEN, 2), np.arange(1, LEN, 2)])
    theta = np.pi * (freq[:, None] + 0.5) * np.arange(LEN)[None, :] / LEN
    forward = np.concatenate([np.cos(theta), -np.sin(theta)], axis=0)
    inverse = (forward.T / LEN).astype(BF16)
    nodes, basis = lagrange(LEN, NODES)
    fwd = np.concatenate([forward, basis[::-1].T], axis=0)
    fwd = np.concatenate(halves(fwd), axis=1)
    tap_high, tap_low = halves(forward @ basis)
    taps = np.concatenate([tap_high, tap_low, tap_high], axis=1)
    near_high, near_low = halves(basis)
    near = np.concatenate([near_high, near_low, near_high], axis=1)
    group = np.arange(width)[None, :] // 16 == np.arange(width // 16)[:, None]
    packed, spans, start = [], [], 0
    for table in (fwd, inverse, near, taps, group):
        table = np.asarray(table, BF16)
        height, depth = table.shape
        spans.append((start, start + height, depth))
        packed.append(np.pad(table, ((0, 0), (0, 2 * LEN - depth))))
        start += height
    return nodes, np.concatenate(packed, axis=0), spans


def table_at(packed_ref, span):
    first, last, depth = span
    return packed_ref[first:last, :depth]


def dot(a, b):
    return lax.dot_general(a, b, (((1,), (0,)), ((), ())), preferred_element_type=F32)


def tripled(values):
    high = values.astype(BF16)
    low = (values - high.astype(F32)).astype(BF16)
    return jnp.concatenate([high, high, low], axis=0)


def twice(values):
    return jnp.concatenate([values, values], axis=0)


def times(re, im, filter_re, filter_im):
    return jnp.concatenate(
        [
            (re * filter_re - im * filter_im).astype(BF16),
            (re * filter_im + im * filter_re).astype(BF16),
        ],
        axis=0,
    )


def column(values):
    rows = lax.broadcasted_iota(jnp.int32, (len(values), 1), 0)
    total = jnp.zeros((len(values), 1), F32)
    for k, value in enumerate(values):
        total = jnp.where(rows == k, np.float32(value), total)
    return total


def weighted(rows_ref, base, weights):
    total = None
    for m in range(weights.shape[0]):
        first = base + m * NODES
        part = rows_ref[first : first + NODES, :] * weights[m : m + 1]
        total = part if total is None else total + part
    return total


def prepare_kernel(nodes, spans, filt_ref, modal_ref, packed_ref, out_ref):
    fwd = table_at(packed_ref, spans[0])[: 2 * LEN]
    modes = modal_ref.shape[0] // 2
    decay = modal_ref[:modes, :]
    residue = modal_ref[modes:, :]
    node_col = column(nodes)
    base = 4 * LEN
    end = base + modes * NODES
    for m in range(modes):
        out_ref[base + m * NODES : base + (m + 1) * NODES, :] = jnp.exp(-node_col * decay[m : m + 1])
    for k, node in enumerate(nodes):
        out_ref[end + k * modes : end + (k + 1) * modes, :] = jnp.exp(-np.float32(node) * decay)
    filters = CHUNK // 16
    expanded = jnp.concatenate(
        [
            lax.dot_general(
                filt_ref[i * filters : (i + 1) * filters, :],
                table_at(packed_ref, spans[4]),
                (((0,), (0,)), ((), ())),
                preferred_element_type=F32,
            ).astype(BF16)
            for i in range(decay.shape[1] // CHUNK)
        ],
        axis=1,
    )
    out_ref[: 2 * LEN, :] = dot(fwd, twice(expanded))
    out_ref[2 * LEN : 4 * LEN, :] = dot(
        table_at(packed_ref, spans[3]), tripled(weighted(out_ref, base, residue))
    )


def near_chunk(
    spans, q_ref, k_ref, v_ref, halo_ref, key_ref, modal_ref, prepared_ref, packed_ref,
    out_ref,
):
    blocks = q_ref.shape[0] // LEN
    half = LEN // 2
    modes = modal_ref.shape[0] // 2
    fwd_all = table_at(packed_ref, spans[0])
    fwd = fwd_all[: 2 * LEN]
    inv = table_at(packed_ref, spans[1])
    near = table_at(packed_ref, spans[2])
    base = 4 * LEN
    end = base + modes * NODES
    decay = modal_ref[:modes, :]
    weight = modal_ref[modes:, :] * jnp.exp(-decay)
    step = jnp.exp(-np.float32(LEN) * decay)
    spectra = [dot(fwd, twice(halo_ref[...]))]
    for i in range(blocks):
        rows = pl.ds(i * LEN, LEN)
        product = (k_ref[rows, :].astype(F32) * v_ref[rows, :].astype(F32)).astype(BF16)
        spectra.append(dot(fwd, twice(product)))
    convolved = []
    for before, now in zip(spectra[:-1], spectra[1:]):
        turned_re = jnp.concatenate(
            [
                now[:half] - before[LEN : LEN + half],
                now[half:LEN] + before[LEN + half :],
            ],
            axis=0,
        )
        turned_im = jnp.concatenate(
            [
                now[LEN : LEN + half] + before[:half],
                now[LEN + half :] - before[half:LEN],
            ],
            axis=0,
        )
        short_re, short_im = prepared_ref[:LEN, :], prepared_ref[LEN : 2 * LEN, :]
        convolved.append(dot(inv, times(turned_re, turned_im, short_re, short_im)))
    seen = []
    for i in range(blocks):
        rows = pl.ds(i * LEN, LEN)
        li_input = key_ref[rows, :].astype(F32) * (q_ref[rows, :].astype(F32) * convolved[i])
        seen.append(dot(fwd_all, twice(li_input.astype(BF16))))
    state = None
    for i in range(blocks):
        rows = pl.ds(i * LEN, LEN)
        long_re = prepared_ref[2 * LEN : 3 * LEN, :]
        long_im = prepared_ref[3 * LEN : 4 * LEN, :]
        value = dot(inv, times(seen[i][:LEN], seen[i][LEN : 2 * LEN], long_re, long_im))
        if state is not None:
            value = value + dot(near, tripled(weighted(prepared_ref, base, weight * state)))
        out_ref[rows, :] = value
        ended = None
        for k in range(NODES):
            first = end + k * modes
            weights = prepared_ref[first : first + modes, :]
            part = weights * seen[i][2 * LEN + k : 2 * LEN + k + 1]
            ended = part if ended is None else ended + part
        state = ended if state is None else step * state + ended
    return state


def far_tile(spans, value_ref, query_ref, state, modal_ref, node_ref, packed_ref, out_ref):
    modes = modal_ref.shape[0] // 2
    decay = modal_ref[:modes, :]
    near = table_at(packed_ref, spans[2])
    step = jnp.exp(-np.float32(LEN) * decay)
    start = modal_ref[modes:, :] * jnp.exp(-decay) * state
    for i in range(query_ref.shape[0] // LEN):
        rows = pl.ds(i * LEN, LEN)
        long_conv = value_ref[rows, :] + dot(near, tripled(weighted(node_ref, 0, start)))
        out_ref[rows, :] = (query_ref[rows, :].astype(F32) * long_conv).astype(BF16)
        start = step * start


def main_kernel(
    spans, count, tiles, q_ref, k_ref, v_ref, halo_ref, key_ref, modal_ref, prepared_ref,
    packed_ref, all_ref, query_ref, node_ref, out_ref, values, ended, got, starts, landed,
    send_one, recv_one, send_two, recv_two,
):
    turn_now = pl.program_id(0)
    mine = lax.axis_index("ctx")
    tokens, width = q_ref.shape
    modes, share = got.shape[1:]
    per = width // share

    def copy(source, target, send, recv, slot, k):
        return pltpu.make_async_remote_copy(
            src_ref=source.at[k],
            dst_ref=target.at[slot],
            send_sem=send.at[k],
            recv_sem=recv.at[slot],
            device_id={"ctx": k},
            device_id_type=pl.DeviceIdType.MESH,
        )

    def first(k):
        return copy(ended, got, send_one, recv_one, mine, k)

    def second(k):
        return copy(starts, landed, send_two, recv_two, mine, k)

    def arrived(buffer, sem, k):
        return copy(buffer, buffer, sem, sem, k, k)

    def other(k):
        return lax.rem(mine + k, count)

    @pl.when(turn_now == 0)
    def _():
        barrier = pltpu.get_barrier_semaphore()

        @pl.loop(1, count)
        def _(k):
            pl.semaphore_signal(
                barrier, inc=1, device_id={"ctx": other(k)}, device_id_type=pl.DeviceIdType.MESH
            )

        pl.semaphore_wait(barrier, count - 1)

    @pl.when(turn_now < tiles)
    def _():
        refs = [q_ref, k_ref, v_ref, halo_ref, key_ref, modal_ref, prepared_ref]
        states = []
        for i in range(width // CHUNK):
            columns = slice(i * CHUNK, (i + 1) * CHUNK)
            parts = [ref.at[:, columns] for ref in refs]
            states.append(
                near_chunk(spans, *parts, packed_ref, values.at[turn_now, :, columns])
            )
        state = jnp.concatenate(states, axis=1)
        for i in range(per):
            owner = turn_now * per + i
            ended[owner] = state[:, i * share : (i + 1) * share]

            @pl.when(owner != mine)
            def _():
                first(owner).start()

    own = lax.div(mine, per)

    @pl.when(turn_now == own + 3)
    def _():
        columns = pl.ds(pl.multiple_of(mine * share, share), share)
        own_decay = jnp.exp(-np.float32(tokens) * all_ref[:modes, columns])
        got[mine] = ended[mine]

        def turn(k, running):
            starts[k] = running

            @pl.when(k != mine)
            def _():
                second(k).start()
                arrived(got, recv_one, k).wait_recv()

            return own_decay * running + got[k]

        lax.fori_loop(0, count, turn, jnp.zeros((modes, share), F32))
        landed[mine] = starts[mine]

    @pl.when(turn_now >= tiles)
    def _():
        tile = turn_now - tiles
        for i in range(per):
            owner = tile * per + i

            @pl.when(owner != mine)
            def _():
                arrived(landed, recv_two, owner).wait_recv()

        state = jnp.concatenate([landed[tile * per + i] for i in range(per)], axis=1)
        far_tile(
            spans, values.at[tile], query_ref, state, modal_ref, node_ref, packed_ref, out_ref
        )

    @pl.when(turn_now == 2 * tiles - 1)
    def _():
        @pl.loop(1, count)
        def _(k):
            first(other(k)).wait_send()
            second(other(k)).wait_send()


def per_device(mr_qkv, mr_filter, li_gates, decay, residue):
    rows = mr_qkv.shape[0]
    channels = mr_qkv.shape[1] // 3
    modes = decay.shape[1]
    count = lax.axis_size("ctx")
    edge = (
        mr_qkv[rows - LEN :, channels : 2 * channels].astype(F32)
        * mr_qkv[rows - LEN :, 2 * channels :].astype(F32)
    ).astype(BF16)
    halo = lax.ppermute(edge, "ctx", [(i - 1, i) for i in range(1, count)])
    modal = jnp.concatenate([decay.T, residue.T], axis=0)

    width = 512
    tiles = channels // width
    nodes, packed, spans = tables(CHUNK)
    packed = jnp.asarray(packed)
    whole = lambda c: pl.BlockSpec(c.shape, lambda j: (0, 0))
    part = lambda height, k=0: pl.BlockSpec((height, width), lambda j, k=k: (0, k * tiles + j))
    shape = lambda height: jax.ShapeDtypeStruct((height, channels), F32)
    params = pltpu.CompilerParams(vmem_limit_bytes=48 * 2**20)
    height = 4 * LEN + 2 * modes * NODES
    prepared = pl.pallas_call(
        functools.partial(prepare_kernel, nodes, spans),
        grid=(tiles,),
        in_specs=[
            pl.BlockSpec((width // 16, LEN), lambda j: (j, 0)), part(2 * modes), whole(packed)
        ],
        out_specs=part(height),
        out_shape=shape(height),
        compiler_params=params,
        name="prepare",
    )(mr_filter, modal, packed)
    def held(height, k=0):
        def place(j):
            return 0, k * tiles + j - lax.div(j, tiles) * (j - tiles + 1)

        return pl.BlockSpec((height, width), place)

    def later(height, k=0):
        return pl.BlockSpec((height, width), lambda j: (k, lax.div(j, tiles) * (j - tiles)))

    share = channels // count
    slots = pltpu.VMEM((count, modes, share), F32)
    return pl.pallas_call(
        functools.partial(main_kernel, spans, count, tiles),
        grid=(2 * tiles,),
        in_specs=[
            held(rows, 0), held(rows, 1), held(rows, 2), held(LEN), held(rows, 1),
            pl.BlockSpec((2 * modes, width), lambda j: (0, lax.rem(j, tiles))),
            held(height), whole(packed), whole(modal), later(rows),
            later(modes * NODES, 4 * LEN // (modes * NODES)),
        ],
        out_specs=later(rows),
        out_shape=jax.ShapeDtypeStruct((rows, channels), BF16),
        scratch_shapes=[pltpu.VMEM((tiles, rows, width), F32)]
        + [slots] * 4
        + [pltpu.SemaphoreType.DMA((count,))] * 4,
        compiler_params=pltpu.CompilerParams(
            vmem_limit_bytes=52 * 2**20, collective_id=0, has_side_effects=True
        ),
        name="main",
    )(
        mr_qkv, mr_qkv, mr_qkv, halo, li_gates, modal, prepared, packed, modal, li_gates, prepared
    )


def solution(mesh):
    return jax.shard_map(
        per_device,
        mesh=mesh,
        in_specs=(P(("groups", "ctx"), None), P(), P(("groups", "ctx"), None), P(), P()),
        out_specs=P(("groups", "ctx"), None),
        check_vma=False,
    )
```
